32 devices in a mesh: groups: 2 (over y), blk: 16 (over z, x, core).
Axes of the slice: x: 2, y: 2, z: 4, core: 2. Of those that a mesh axis runs over, the one named last changes fastest.
Arguments:
- test_points: bfloat16 [48, 98304], P(None, ('groups', 'blk')), parts along dimension 1, may hold values from -6 to 6
- train_points: bfloat16 [48, 16384], P(None, ('groups', 'blk')), parts along dimension 1, may hold values from -6 to 6
- update_columns: bfloat16 [64, 16384], P(None, ('groups', 'blk')), parts along dimension 1, may hold values from -0.25 to 0.25
- pattern: int32 [192, 16], P('groups'), parts along dimension 0, may hold values from -1 to 15, as said below
- lengthscales: float32 [96], P('groups'), parts along dimension 0, may hold values from 4 to 16
- frequencies: bfloat16 [48, 256], P(None, 'blk'), may hold values from -12 to 12
- phases: bfloat16 [1, 256], P(None, 'blk'), may hold values from 0 to 6.28125
- prior_weights: bfloat16 [64, 256], P(None, 'blk'), may hold values from -6 to 6
Outputs:
- samples: float32 [64, 98304], P(None, ('groups', 'blk')), parts along dimension 1
The draws below stay inside these ranges and needn't reach their ends.
There are 2 independent parts, one for each index of `groups`. The reference program is written for one: setup_inputs(seed, part) draws one part's arguments, and reference() takes and returns one part's arrays. A program takes and returns all parts, laid end to end along the dimension named above; an argument that names none is the same for every part. Nothing has to cross between parts.
Inputs may be any that keep to these rules, and one draw needn't show every extreme that they name: `pattern`: row t lists distinct training blocks of 0 to 15 in its first slots and -1 in the rest; every row has one tile or more, and some row fills all 16 slots.
All inputs are finite; a program needn't handle non-finite values.
Results may differ from the reference program's by a relative error of at most 0.004.
Values may be sent and summed in bfloat16 or wider, within the bound.
A program may use at most 128 MiB of HBM per device.

```python
import math
import jax
import jax.numpy as jnp
from jax import lax

F = 48
S = 64
TB = 512
TEST_DEV = 6
MOST = 16
NF = 256
TEST_BLOCKS = 96
NTEST = 49152
NTRAIN = 8192
N_BLK = 16


def draw_pattern(key, part):
    key = jax.random.fold_in(key, 5)
    keys = jax.random.split(key, 5)
    rows = TEST_DEV * N_BLK
    column_ids = jnp.arange(N_BLK, dtype=jnp.int32)
    home = jnp.arange(rows, dtype=jnp.int32) // TEST_DEV
    apart = jnp.abs(column_ids[None, :] - home[:, None])
    apart = jnp.minimum(apart, N_BLK - apart)
    scores = jax.random.randint(keys[0], (rows, N_BLK), 0, N_BLK, dtype=jnp.int32) + apart
    scores = scores * N_BLK + column_ids[None, :]
    order = jnp.argsort(scores, axis=1, stable=True).astype(jnp.int32)
    chosen = order[:, :MOST]
    first = jax.random.randint(keys[1], (N_BLK,), 0, 4, dtype=jnp.int32)
    second = jax.random.randint(keys[2], (N_BLK,), 0, 4, dtype=jnp.int32)
    level = jnp.repeat(first * second // 3, TEST_DEV)
    extra = jax.random.randint(keys[3], (rows,), 0, MOST // 4 + 1, dtype=jnp.int32)
    counts = jnp.minimum(MOST, jnp.maximum(1, MOST // 4 + level * (MOST // 4) + extra))
    full_row = jax.random.randint(keys[4], (), 0, rows, dtype=jnp.int32)
    counts = jnp.where(jnp.arange(rows, dtype=jnp.int32) == full_row, MOST, counts)
    slots = jnp.arange(MOST, dtype=jnp.int32)
    return jnp.where(slots[None, :] < counts[:, None], chosen, -1).astype(jnp.int32)


def draw_frequencies(key, part):
    key = jax.random.fold_in(key, 7)
    key_normal, key_gamma = jax.random.split(key)
    normal_part = jax.random.normal(key_normal, (F, NF), jnp.float32)
    chi_square = jnp.maximum(2.0 * jax.random.gamma(key_gamma, 2.5, (F, NF), jnp.float32), 0.5)
    values = jnp.clip(normal_part * jnp.sqrt(5.0 / chi_square), -12.0, 12.0)
    return values.astype(jnp.bfloat16)


def steps_of(rng, dims, cuts, least, top_value):
    level = 1.0
    for position, shards_of in cuts:
        draws = jax.random.uniform(jax.random.fold_in(jax.random.fold_in(rng, 6), position), (shards_of,), jnp.float32, least / len(cuts), top_value / len(cuts))
        level = level * jnp.repeat(jnp.exp(draws), dims[position] // shards_of).reshape((-1,) + (1,) * (len(dims) - 1 - position))
    return level


def bell_draw(stream_key, dims, deviation, bound, cuts=(), held_as=jnp.bfloat16):
    array = jax.random.normal(stream_key, dims, jnp.float32) * deviation
    if len(cuts) > 0:
        array = steps_of(stream_key, dims, cuts, -0.22, 0.18) * array
    return jnp.clip(array, min=-bound, max=bound).astype(held_as)


def setup_inputs(seed: int = 0, part: int = 0) -> dict:
    arg_keys = jax.random.split(jax.random.key(seed), 9)
    part_keys = jax.random.split(jax.random.fold_in(arg_keys[8], part), 9)
    return {
        "test_points": bell_draw(part_keys[0], (F, NTEST), 1.0, 6.0, ((1, 16),)),
        "train_points": bell_draw(part_keys[1], (F, NTRAIN), 1.0, 6.0, ((1, 16),)),
        "update_columns": bell_draw(part_keys[2], (S, NTRAIN), 0.03, 0.25, ((1, 16),)),
        "pattern": draw_pattern(jax.random.fold_in(jax.random.fold_in(arg_keys[8], part), 71), part),
        "lengthscales": jnp.clip(jnp.exp(jax.random.uniform(part_keys[4], (F,), jnp.float32, math.log(4.0), math.log(16.0))), 4.0, 16.0),
        "frequencies": draw_frequencies(jax.random.fold_in(arg_keys[8], 71), part),
        "phases": jnp.clip(6.28125 * jax.random.uniform(arg_keys[6], (1, NF), jnp.float32) ** steps_of(arg_keys[6], (1, NF), ((1, 16),), -0.2, 0.2), 0.0, 6.28125).astype(jnp.bfloat16),
        "prior_weights": bell_draw(arg_keys[7], (S, NF), 1.0, 6.0, ((1, 16),)),
    }


def matern_tile(train_block, test_block):
    train_wide = train_block.astype(jnp.float32)
    test_wide = test_block.astype(jnp.float32)
    cross = lax.dot_general(train_wide, test_wide, (((0,), (0,)), ((), ())), precision=lax.Precision.HIGHEST)
    train_norm = lax.optimization_barrier(jnp.sum(train_wide * train_wide, axis=0))
    test_norm = lax.optimization_barrier(jnp.sum(test_wide * test_wide, axis=0))
    dist_sq = jnp.maximum(train_norm[:, None] + test_norm[None, :] - 2.0 * cross, 0.0)
    scaled = jnp.sqrt(5.0 * dist_sq)
    return ((1.0 + scaled + scaled * scaled / 3.0) * jnp.exp(-scaled)).astype(jnp.bfloat16)

def reference(test_points, train_points, update_columns, pattern, lengthscales, frequencies, phases, prior_weights):
    test_scaled = (test_points.astype(jnp.float32) / lengthscales[:, None]).astype(jnp.bfloat16)
    train_scaled = (train_points.astype(jnp.float32) / lengthscales[:, None]).astype(jnp.bfloat16)
    freq_wide = frequencies.astype(jnp.float32)
    phase_wide = phases[0].astype(jnp.float32)
    weight_wide = prior_weights.astype(jnp.float32)

    def block_update(block):
        test_block = lax.dynamic_slice_in_dim(test_scaled, block * TB, TB, 1)

        def slot_step(slot, running):
            index = pattern[block, slot]

            def compute(value):
                begin = (jnp.maximum(index, 0) * TB).astype(jnp.int32)
                train_block = lax.dynamic_slice_in_dim(train_scaled, begin, TB, 1)
                columns = lax.dynamic_slice_in_dim(update_columns, begin, TB, 1).astype(jnp.float32)
                kernel = matern_tile(train_block, test_block).astype(jnp.float32)
                return value + jnp.dot(columns, kernel, precision=lax.Precision.HIGHEST)
            return lax.cond(index >= 0, compute, lambda value: value, running)
        update = lax.fori_loop(0, MOST, slot_step, jnp.zeros((S, TB), jnp.float32))
        proj = jnp.dot(freq_wide.T, test_block.astype(jnp.float32), precision=lax.Precision.HIGHEST)
        features = jnp.cos(proj + phase_wide[:, None]).astype(jnp.bfloat16).astype(jnp.float32)
        prior = math.sqrt(2.0 / NF) * jnp.dot(weight_wide, features, precision=lax.Precision.HIGHEST)
        return prior + update
    blocks = lax.map(block_update, jnp.arange(TEST_BLOCKS, dtype=jnp.int32))
    return jnp.transpose(blocks, (1, 0, 2)).reshape(S, NTEST)
```

```python
import functools
import math

import jax
import jax.numpy as jnp
from jax import lax
from jax.experimental import pallas as pl
from jax.experimental.pallas import tpu as pltpu
from jax.sharding import PartitionSpec as P

TB = 512
PADDED = 128
MESH = pl.DeviceIdType.MESH
LOG2E = math.log2(math.e)
COS_TERMS = [(-1.0) ** k * (2.0 * math.pi) ** (2 * k) / math.factorial(2 * k) for k in range(11)]


def three_parts(value):
    high = value.astype(jnp.bfloat16).astype(jnp.float32)
    rest = value - high
    middle = rest.astype(jnp.bfloat16).astype(jnp.float32)
    return high, middle, (rest - middle).astype(jnp.bfloat16).astype(jnp.float32)


def rows_of(first, second):
    width = first[0].shape[1] if hasattr(first[0], "shape") else second[0].shape[1]
    row = lax.broadcasted_iota(jnp.int32, (32, width), 0)
    out = jnp.zeros((32, width), jnp.float32)
    for place, part in enumerate(list(first) + list(second)):
        out = jnp.where(row == place, part, out)
    return out


def turn_cos(turns):
    f = turns - jnp.round(turns)
    z = f * f
    total = jnp.full_like(z, COS_TERMS[-1])
    for term in COS_TERMS[-2::-1]:
        total = total * z + term
    return total


def gather_kernel(
    n, test_ref, train_ref, columns_ref, scale_ref, pack_ref,
    train_aug, all_columns, test_aug, prior_ref,
    packs, blocks, small_send, small_recv, big_send, big_recv,
):
    group = lax.axis_index("groups")
    me = lax.axis_index("blk")
    feats, samples = train_ref.shape[0], columns_ref.shape[0]
    depth = pack_ref.shape[0]
    lines = n // 4
    a, b, c = me // 4, (me // 2) % 2, me % 2

    def index(a_, b_, c_):
        return (a_ * 2 + b_) * 2 + c_

    line = [index((a + k) % lines, b, c) for k in range(lines)]
    across = index(a, 1 - b, c)
    core = index(a, b, 1 - c)
    partners = line[1:] + [across, core]

    barrier = pltpu.get_barrier_semaphore()
    for other in partners:
        pl.semaphore_signal(barrier, inc=1, device_id=(group, other), device_id_type=MESH)

    scale = scale_ref[...]
    train = (train_ref[...].astype(jnp.float32) / scale).astype(jnp.bfloat16)
    blocks[pl.ds(me, 1), :feats, :] = train[None]
    blocks[pl.ds(me, 1), feats:, :] = columns_ref[...][None]
    packs[pl.ds(me, 1)] = pack_ref[...][None]
    pl.semaphore_wait(barrier, len(partners))

    def copy(buffer, send, recv, source, target, number):
        return pltpu.make_async_remote_copy(
            src_ref=buffer.at[pl.ds(source, 1)], dst_ref=buffer.at[pl.ds(source, 1)],
            send_sem=send.at[number], recv_sem=recv.at[source],
            device_id=(group, target), device_id_type=MESH,
        )

    sent = []

    def start(small, source, target):
        number = counts[small]
        counts[small] += 1
        one = (copy(packs, small_send, small_recv, source, target, number) if small
               else copy(blocks, big_send, big_recv, source, target, number))
        one.start()
        sent.append(one)

    def arrive(small, source):
        if small:
            copy(packs, small_send, small_recv, source, me, 0).wait_recv()
        else:
            copy(blocks, big_send, big_recv, source, me, 0).wait_recv()

    counts = {True: 0, False: 0}

    def first_wave(small):
        for other in line[1:]:
            start(small, me, other)
        start(small, me, across)
        start(small, me, core)

    def line_arrivals(small):
        for k in range(1, lines):
            source = line[lines - k]
            arrive(small, source)
            start(small, source, across)
            start(small, source, core)

    def across_arrivals(small):
        for k in range(lines):
            source = index((a - k) % lines, 1 - b, c)
            arrive(small, source)
            start(small, source, core)

    def core_arrivals(small):
        for k in range(lines):
            arrive(small, index((a - k) % lines, b, 1 - c))
            arrive(small, index((a - k) % lines, 1 - b, 1 - c))

    first_wave(True)
    first_wave(False)

    chunks = test_ref.shape[1] // TB

    def make_test(i, _):
        at = pl.ds(pl.multiple_of(i * TB, TB), TB)
        scaled = (test_ref[:, at].astype(jnp.float32) / scale).astype(jnp.bfloat16)
        wide = scaled.astype(jnp.float32)
        norm = 5.0 * jnp.sum(wide * wide, axis=0, keepdims=True)
        tail = rows_of([1.0, 1.0, 1.0], three_parts(norm))
        test_aug[:feats, at] = scaled
        test_aug[feats:2 * feats, at] = scaled
        test_aug[2 * feats:, at] = tail.astype(jnp.bfloat16)
        return 0

    lax.fori_loop(0, chunks, make_test, 0)

    line_arrivals(True)
    across_arrivals(True)
    core_arrivals(True)
    line_arrivals(False)

    total = n * depth
    factor = math.sqrt(2.0 / total)
    step = min(total, 256)
    held = step // depth

    def make_prior(i, _):
        at = pl.ds(pl.multiple_of(i * TB, TB), TB)

        def part(first):
            pack = packs[pl.ds(first, held)].reshape(step, 2 * PADDED)
            turns = jnp.dot(
                pack[:, :PADDED], test_aug[:, at], preferred_element_type=jnp.float32
            ) * (0.5 / math.pi)
            features = turn_cos(turns).astype(jnp.bfloat16)
            return lax.dot_general(
                pack[:, PADDED:], features, (((0,), (0,)), ((), ())),
                preferred_element_type=jnp.float32,
            )[:samples]

        if total == step:
            result = part(0)
        else:
            result = lax.fori_loop(
                0, total // step, lambda p, run: run + part(p * held),
                jnp.zeros((samples, TB), jnp.float32),
            )
        prior_ref[:, at] = result * factor
        return 0

    lax.fori_loop(0, chunks, make_prior, 0)

    across_arrivals(False)
    core_arrivals(False)

    def make_train(s, _):
        block = blocks[pl.ds(s, 1)][0]
        wide = block[:feats].astype(jnp.float32)
        norm = 5.0 * jnp.sum(wide * wide, axis=0, keepdims=True)
        double = -10.0 * wide
        high = double.astype(jnp.bfloat16).astype(jnp.float32)
        tail = rows_of(three_parts(norm), [1.0, 1.0, 1.0])
        whole = jnp.concatenate([high, double - high, tail], axis=0)
        train_aug[pl.ds(s, 1)] = whole.T.astype(jnp.bfloat16)[None]
        all_columns[pl.ds(s, 1)] = block[feats:][None]
        return 0

    lax.fori_loop(0, n, make_train, 0)
    for one in sent:
        one.wait_send()


def tile_kernel(pattern_ref, train_aug, all_columns, test_aug, prior_ref, out_ref):
    me = lax.axis_index("blk")
    rows = test_aug.shape[1] // TB
    slots = pattern_ref.shape[1]
    half = 256

    def one_row(row, _):
        line = me * rows + row
        start = pl.multiple_of(row * TB, TB)
        at = pl.ds(start, TB)
        out_ref[:, at] = prior_ref[:, at]

        def more(slot):
            return jnp.logical_and(
                slot < slots, pattern_ref[line, jnp.minimum(slot, slots - 1)] >= 0
            )

        def tile(slot):
            j = pattern_ref[line, slot]
            for part in range(TB // half):
                here = pl.ds(pl.multiple_of(start + part * half, half), half)
                dist = jnp.dot(
                    train_aug[j], test_aug[:, here], preferred_element_type=jnp.float32
                )
                dist = jnp.maximum(dist, 1e-30)
                q = dist * lax.rsqrt(dist)
                bell = jnp.exp2(q * (-LOG2E))
                tile_value = (((q * (1.0 / 3.0) + 1.0) * q + 1.0) * bell).astype(jnp.bfloat16)
                out_ref[:, here] += jnp.dot(
                    all_columns[j], tile_value, preferred_element_type=jnp.float32
                )
            return slot + 1

        lax.while_loop(more, tile, 0)
        return 0

    lax.fori_loop(0, rows, one_row, 0)


def on_device(
    test_points, train_points, update_columns, pattern, lengthscales, frequencies, phases,
    prior_weights,
):
    n = lax.axis_size("blk")
    feats, points = test_points.shape
    samples = update_columns.shape[0]
    depth = frequencies.shape[1]
    pack = jnp.concatenate(
        [
            frequencies.T, jnp.zeros((depth, feats), jnp.bfloat16), phases.T,
            jnp.zeros((depth, PADDED - 2 * feats - 1), jnp.bfloat16), prior_weights.T,
            jnp.zeros((depth, PADDED - samples), jnp.bfloat16),
        ],
        axis=1,
    )
    vmem = pl.BlockSpec(memory_space=pltpu.VMEM)
    copies = n // 4 + 1 + 2 * (n // 4 - 1) + n // 4
    train_aug, all_columns, test_aug, prior = pl.pallas_call(
        functools.partial(gather_kernel, n),
        out_shape=(
            jax.ShapeDtypeStruct((n, TB, PADDED), jnp.bfloat16),
            jax.ShapeDtypeStruct((n, samples, TB), jnp.bfloat16),
            jax.ShapeDtypeStruct((PADDED, points), jnp.bfloat16),
            jax.ShapeDtypeStruct((samples, points), jnp.float32),
        ),
        in_specs=[vmem] * 5,
        out_specs=(vmem,) * 4,
        scratch_shapes=[
            pltpu.VMEM((n, depth, 2 * PADDED), jnp.bfloat16),
            pltpu.VMEM((n, feats + samples, TB), jnp.bfloat16),
            pltpu.SemaphoreType.DMA((copies,)),
            pltpu.SemaphoreType.DMA((n,)),
            pltpu.SemaphoreType.DMA((copies,)),
            pltpu.SemaphoreType.DMA((n,)),
        ],
        compiler_params=pltpu.CompilerParams(
            collective_id=0, has_side_effects=True, vmem_limit_bytes=56 * 2**20
        ),
        name="gather_and_prior",
    )(test_points, train_points, update_columns, lengthscales[:, None], pack)
    return pl.pallas_call(
        tile_kernel,
        out_shape=jax.ShapeDtypeStruct((samples, points), jnp.float32),
        in_specs=[pl.BlockSpec(memory_space=pltpu.SMEM)] + [vmem] * 4,
        out_specs=vmem,
        compiler_params=pltpu.CompilerParams(vmem_limit_bytes=56 * 2**20),
        name="tiles",
    )(pattern, train_aug, all_columns, test_aug, prior)


def solution(mesh):
    placed = (
        P(None, ("groups", "blk")),
        P(None, ("groups", "blk")),
        P(None, ("groups", "blk")),
        P("groups", None),
        P("groups"),
        P(None, "blk"),
        P(None, "blk"),
        P(None, "blk"),
    )
    return jax.shard_map(
        on_device, mesh=mesh, in_specs=placed, out_specs=P(None, ("groups", "blk")), check_vma=False
    )
```

```python
import functools
import math

import jax
import jax.numpy as jnp
from jax import lax
from jax.experimental import pallas as pl
from jax.experimental.pallas import tpu as pltpu
from jax.sharding import PartitionSpec as P

TB = 512
PADDED = 128
MESH = pl.DeviceIdType.MESH
LOG2E = math.log2(math.e)
COS_TERMS = [(-1.0) ** k * (2.0 * math.pi) ** (2 * k) / math.factorial(2 * k) for k in range(11)]


def three_parts(value):
    high = value.astype(jnp.bfloat16).astype(jnp.float32)
    rest = value - high
    middle = rest.astype(jnp.bfloat16).astype(jnp.float32)
    return high, middle, (rest - middle).astype(jnp.bfloat16).astype(jnp.float32)


def rows_of(first, second):
    width = first[0].shape[1] if hasattr(first[0], "shape") else second[0].shape[1]
    row = lax.broadcasted_iota(jnp.int32, (32, width), 0)
    out = jnp.zeros((32, width), jnp.float32)
    for place, part in enumerate(list(first) + list(second)):
        out = jnp.where(row == place, part, out)
    return out


def turn_cos(turns):
    f = turns - jnp.round(turns)
    z = f * f
    total = jnp.full_like(z, COS_TERMS[-1])
    for term in COS_TERMS[-2::-1]:
        total = total * z + term
    return total


def gather_kernel(
    n, test_ref, train_ref, columns_ref, scale_ref, pack_ref,
    train_aug, all_columns, test_aug, prior_ref,
    packs, blocks, small_send, small_recv, big_send, big_recv,
):
    group = lax.axis_index("groups")
    me = lax.axis_index("blk")
    feats, samples = train_ref.shape[0], columns_ref.shape[0]
    depth = pack_ref.shape[0]
    lines = n // 4
    a, b, c = me // 4, (me // 2) % 2, me % 2

    def index(a_, b_, c_):
        return (a_ * 2 + b_) * 2 + c_

    line = [index((a + k) % lines, b, c) for k in range(lines)]
    across = index(a, 1 - b, c)
    core = index(a, b, 1 - c)
    partners = line[1:] + [across, core]

    barrier = pltpu.get_barrier_semaphore()
    for other in partners:
        pl.semaphore_signal(barrier, inc=1, device_id=(group, other), device_id_type=MESH)

    scale = scale_ref[...]
    train = (train_ref[...].astype(jnp.float32) / scale).astype(jnp.bfloat16)
    blocks[pl.ds(me, 1), :feats, :] = train[None]
    blocks[pl.ds(me, 1), feats:, :] = columns_ref[...][None]
    packs[pl.ds(me, 1)] = pack_ref[...][None]
    pl.semaphore_wait(barrier, len(partners))

    def copy(buffer, send, recv, source, target, number):
        return pltpu.make_async_remote_copy(
            src_ref=buffer.at[pl.ds(source, 1)], dst_ref=buffer.at[pl.ds(source, 1)],
            send_sem=send.at[number], recv_sem=recv.at[source],
            device_id=(group, target), device_id_type=MESH,
        )

    sent = []

    def start(small, source, target):
        number = counts[small]
        counts[small] += 1
        one = (copy(packs, small_send, small_recv, source, target, number) if small
               else copy(blocks, big_send, big_recv, source, target, number))
        one.start()
        sent.append(one)

    def arrive(small, source):
        if small:
            copy(packs, small_send, small_recv, source, me, 0).wait_recv()
        else:
            copy(blocks, big_send, big_recv, source, me, 0).wait_recv()

    counts = {True: 0, False: 0}

    def first_wave(small):
        for other in line[1:]:
            start(small, me, other)
        start(small, me, across)
        start(small, me, core)

    def line_arrivals(small):
        for k in range(1, lines):
            source = line[lines - k]
            arrive(small, source)
            start(small, source, across)
            start(small, source, core)

    def across_arrivals(small):
        for k in range(lines):
            source = index((a - k) % lines, 1 - b, c)
            arrive(small, source)
            start(small, source, core)

    def core_arrivals(small):
        for k in range(lines):
            arrive(small, index((a - k) % lines, b, 1 - c))
            arrive(small, index((a - k) % lines, 1 - b, 1 - c))

    first_wave(True)
    first_wave(False)

    chunks = test_ref.shape[1] // TB

    def make_test(i, _):
        at = pl.ds(pl.multiple_of(i * TB, TB), TB)
        scaled = (test_ref[:, at].astype(jnp.float32) / scale).astype(jnp.bfloat16)
        wide = scaled.astype(jnp.float32)
        norm = 5.0 * jnp.sum(wide * wide, axis=0, keepdims=True)
        tail = rows_of([1.0, 1.0, 1.0], three_parts(norm))
        test_aug[:feats, at] = scaled
        test_aug[feats:2 * feats, at] = scaled
        test_aug[2 * feats:, at] = tail.astype(jnp.bfloat16)
        return 0

    lax.fori_loop(0, chunks, make_test, 0)

    line_arrivals(True)
    across_arrivals(True)
    core_arrivals(True)
    line_arrivals(False)

    total = n * depth
    factor = math.sqrt(2.0 / total)
    step = min(total, 256)
    held = step // depth

    def make_prior(i, _):
        at = pl.ds(pl.multiple_of(i * TB, TB), TB)

        def part(first):
            pack = packs[pl.ds(first, held)].reshape(step, 2 * PADDED)
            turns = jnp.dot(
                pack[:, :PADDED], test_aug[:, at], preferred_element_type=jnp.float32
            ) * (0.5 / math.pi)
            features = turn_cos(turns).astype(jnp.bfloat16)
            return lax.dot_general(
                pack[:, PADDED:], features, (((0,), (0,)), ((), ())),
                preferred_element_type=jnp.float32,
            )[:samples]

        if total == step:
            result = part(0)
        else:
            result = lax.fori_loop(
                0, total // step, lambda p, run: run + part(p * held),
                jnp.zeros((samples, TB), jnp.float32),
            )
        prior_ref[:, at] = result * factor
        return 0

    lax.fori_loop(0, chunks, make_prior, 0)

    across_arrivals(False)
    core_arrivals(False)

    def make_train(s, _):
        block = blocks[pl.ds(s, 1)][0]
        wide = block[:feats].astype(jnp.float32)
        norm = 5.0 * jnp.sum(wide * wide, axis=0, keepdims=True)
        double = -10.0 * wide
        high = double.astype(jnp.bfloat16).astype(jnp.float32)
        tail = rows_of(three_parts(norm), [1.0, 1.0, 1.0])
        whole = jnp.concatenate([high, double - high, tail], axis=0)
        train_aug[pl.ds(s, 1)] = whole.T.astype(jnp.bfloat16)[None]
        all_columns[pl.ds(s, 1)] = block[feats:][None]
        return 0

    lax.fori_loop(0, n, make_train, 0)
    for one in sent:
        one.wait_send()


def matern_thrice(dist):
    dist = jnp.maximum(dist, 1e-30)
    q = dist * lax.rsqrt(dist)
    bell = jnp.exp2(q * (-LOG2E)).astype(jnp.bfloat16)
    q = q.astype(jnp.bfloat16)
    three = jnp.bfloat16(3.0)
    return ((q + three) * q + three) * bell


UNROLL = 4


def tile_kernel(
    pattern_ref, train_aug, all_columns, test_aug, prior_ref, out_ref,
    sums, even, odd, row_list, block_list,
):
    me = lax.axis_index("blk")
    rows = test_aug.shape[1] // TB
    slots = pattern_ref.shape[1]

    def list_row(row, count):
        def more(state):
            slot, _ = state
            return jnp.logical_and(
                slot < slots, pattern_ref[me * rows + row, jnp.minimum(slot, slots - 1)] >= 0
            )

        def put(state):
            slot, place = state
            row_list[place] = row
            block_list[place] = pattern_ref[me * rows + row, slot]
            return slot + 1, place + 1

        return lax.while_loop(more, put, (0, count))[1]

    count = lax.fori_loop(0, rows, list_row, 0)
    for extra in range(UNROLL + 1):
        row_list[count + extra] = rows
        block_list[count + extra] = 0
    sums[...] = jnp.zeros_like(sums)

    def front(place, held):
        row = jnp.minimum(row_list[place], rows - 1)
        at = pl.ds(pl.multiple_of(row * TB, TB), TB)
        held[...] = matern_thrice(jnp.dot(
            train_aug[block_list[place]], test_aug[:, at], preferred_element_type=jnp.float32
        ))

    def back(place, held):
        sums[row_list[place]] += jnp.dot(
            all_columns[block_list[place]], held[...], preferred_element_type=jnp.float32
        )

    held = (even, odd)
    front(0, even)

    def step(i, _):
        first = i * UNROLL
        for u in range(UNROLL):
            front(first + u + 1, held[(u + 1) % 2])
            back(first + u, held[u % 2])
        return 0

    lax.fori_loop(0, (count + UNROLL - 1) // UNROLL, step, 0)
    for row in range(rows):
        at = pl.ds(row * TB, TB)
        out_ref[:, at] = prior_ref[:, at] + sums[row] * (1.0 / 3.0)


def as_column(row):
    size = row.shape[1]
    across = lax.broadcasted_iota(jnp.int32, (size, size), 1)
    down = lax.broadcasted_iota(jnp.int32, (size, size), 0)
    return jnp.sum(jnp.where(across == down, row, 0.0), axis=1, keepdims=True)


def dense_kernel(
    n, test_ref, train_ref, columns_ref, scale_ref, freq_ref, phase_ref, weight_ref, pattern_ref,
    out_ref,
    packs, blocks, test_aug, train_aug, sums, masks, even, odd,
    small_send, small_recv, big_send, big_recv,
):
    group = lax.axis_index("groups")
    me = lax.axis_index("blk")
    feats, samples = train_ref.shape[0], columns_ref.shape[0]
    depth = freq_ref.shape[0]
    rows = test_ref.shape[1] // TB
    lines = n // 4
    a, b, c = me // 4, (me // 2) % 2, me % 2

    def index(a_, b_, c_):
        return (a_ * 2 + b_) * 2 + c_

    line = [index((a + k) % lines, b, c) for k in range(lines)]
    across = index(a, 1 - b, c)
    core = index(a, b, 1 - c)
    partners = line[1:] + [across, core]

    barrier = pltpu.get_barrier_semaphore()
    for other in partners:
        pl.semaphore_signal(barrier, inc=1, device_id=(group, other), device_id_type=MESH)

    scale = as_column(scale_ref[...])
    train = (train_ref[...].astype(jnp.float32) / scale).astype(jnp.bfloat16)
    blocks[pl.ds(me, 1), :feats, :] = train[None]
    blocks[pl.ds(me, 1), feats:, :] = columns_ref[...][None]
    lane = lax.broadcasted_iota(jnp.int32, (depth, PADDED), 1)
    phase = as_column(phase_ref[...].astype(jnp.float32))
    pack = jnp.where(lane == 2 * feats, phase, 0.0).astype(jnp.bfloat16)
    packs[pl.ds(me, 1), :, :PADDED] = pack[None]
    packs[pl.ds(me, 1), :, :feats] = freq_ref[...][None]
    packs[pl.ds(me, 1), :, PADDED:] = jnp.zeros((1, depth, PADDED), jnp.bfloat16)
    packs[pl.ds(me, 1), :, PADDED:PADDED + samples] = weight_ref[...][None]
    pl.semaphore_wait(barrier, len(partners))

    def copy(buffer, send, recv, source, target, number):
        return pltpu.make_async_remote_copy(
            src_ref=buffer.at[pl.ds(source, 1)], dst_ref=buffer.at[pl.ds(source, 1)],
            send_sem=send.at[number], recv_sem=recv.at[source],
            device_id=(group, target), device_id_type=MESH,
        )

    def small(source, target, number):
        return copy(packs, small_send, small_recv, source, target, number)

    def big(source, target, number):
        return copy(blocks, big_send, big_recv, source, target, number)

    for number, other in enumerate(partners):
        small(me, other, number).start()
    for number, other in enumerate(partners):
        big(me, other, number).start()
    copies = 4 * lines - 1

    def make_test(i, _):
        at = pl.ds(pl.multiple_of(i * TB, TB), TB)
        scaled = (test_ref[:, at].astype(jnp.float32) / scale).astype(jnp.bfloat16)
        wide = scaled.astype(jnp.float32)
        norm = 5.0 * jnp.sum(wide * wide, axis=0, keepdims=True)
        tail = rows_of([1.0, 1.0, 1.0], three_parts(norm))
        test_aug[:feats, at] = scaled
        test_aug[feats:2 * feats, at] = scaled
        test_aug[2 * feats:, at] = tail.astype(jnp.bfloat16)
        return 0

    lax.fori_loop(0, rows, make_test, 0)

    slots, all_rows = pattern_ref.shape
    wide_pattern = pattern_ref[...].astype(jnp.float32)
    place = lax.broadcasted_iota(jnp.int32, (slots, all_rows), 1)
    number = lax.broadcasted_iota(jnp.int32, (slots, n), 1).astype(jnp.float32)
    for row in range(rows):
        named = jnp.sum(
            jnp.where(place == me * rows + row, wide_pattern, 0.0), axis=1, keepdims=True
        )
        found = jnp.sum(jnp.where(named == number, 1.0 / 3.0, 0.0), axis=0, keepdims=True)
        masks[row] = jnp.broadcast_to(as_column(found), (n, TB))

    sums[...] = jnp.zeros_like(sums)
    odd[...] = jnp.zeros_like(odd)
    held = (even, odd)

    def origin(k):
        kind, far = k // lines, k % lines
        swap_b, swap_c = kind % 2, kind // 2
        return index(
            (a + lines - far) % lines, b + swap_b - 2 * b * swap_b, c + swap_c - 2 * c * swap_c
        )

    def front(row):
        at = pl.ds(row * TB, TB)
        held[row % 2][...] = matern_thrice(
            jnp.dot(train_aug[...], test_aug[:, at], preferred_element_type=jnp.float32)
        )

    def back(source, row):
        product = jnp.dot(
            blocks[pl.ds(source, 1), feats:, :][0], held[row % 2][...],
            preferred_element_type=jnp.float32,
        )
        sums[row] += product * masks[row, pl.ds(source, 1), :]

    def one_block(k, _):
        source = origin(k)
        before = origin(jnp.maximum(k - 1, 0))

        @pl.when(k > 0)
        def _():
            big(source, me, 0).wait_recv()

        @pl.when(jnp.logical_and(k > 0, k < lines))
        def _():
            big(source, across, lines + 2 * k - 1).start()
            big(source, core, lines + 2 * k).start()
            small(source, me, 0).wait_recv()
            small(source, across, lines + 2 * k - 1).start()
            small(source, core, lines + 2 * k).start()

        @pl.when(jnp.logical_and(k >= lines, k < 2 * lines))
        def _():
            big(source, core, 2 * lines - 1 + k).start()
            small(source, me, 0).wait_recv()
            small(source, core, 2 * lines - 1 + k).start()

        @pl.when(k >= 2 * lines)
        def _():
            small(source, me, 0).wait_recv()

        wide = blocks[pl.ds(source, 1), :feats, :][0].astype(jnp.float32)
        norm = 5.0 * jnp.sum(wide * wide, axis=0, keepdims=True)
        double = -10.0 * wide
        high = double.astype(jnp.bfloat16).astype(jnp.float32)
        tail = rows_of(three_parts(norm), [1.0, 1.0, 1.0])
        whole = jnp.concatenate([high, double - high, tail], axis=0)
        train_aug[...] = whole.T.astype(jnp.bfloat16)
        for row in range(rows):
            front(row)
            if row == 0:
                back(before, rows - 1)
            else:
                back(source, row - 1)
        return 0

    lax.fori_loop(0, n, one_block, 0)
    back(origin(n - 1), rows - 1)

    factor = math.sqrt(2.0 / (n * depth))
    every = packs[...].reshape(n * depth, 2 * PADDED)

    def finish(i, _):
        at = pl.ds(pl.multiple_of(i * TB, TB), TB)
        turns = jnp.dot(
            every[:, :PADDED], test_aug[:, at], preferred_element_type=jnp.float32
        ) * (0.5 / math.pi)
        prior = lax.dot_general(
            every[:, PADDED:], turn_cos(turns).astype(jnp.bfloat16), (((0,), (0,)), ((), ())),
            preferred_element_type=jnp.float32,
        )[:samples]
        out_ref[:, at] = prior * factor + sums[pl.ds(i, 1)][0]
        return 0

    lax.fori_loop(0, rows, finish, 0)
    for number in range(copies):
        small(me, core, number).wait_send()
        big(me, core, number).wait_send()


def dense_on_device(
    test_points, train_points, update_columns, pattern, lengthscales, frequencies, phases,
    prior_weights,
):
    n = lax.axis_size("blk")
    feats, points = test_points.shape
    samples = update_columns.shape[0]
    depth = frequencies.shape[1]
    rows = points // TB
    vmem = pl.BlockSpec(memory_space=pltpu.VMEM)
    copies = n - 1
    return pl.pallas_call(
        functools.partial(dense_kernel, n),
        out_shape=jax.ShapeDtypeStruct((samples, points), jnp.float32),
        in_specs=[vmem] * 8,
        out_specs=vmem,
        scratch_shapes=[
            pltpu.VMEM((n, depth, 2 * PADDED), jnp.bfloat16),
            pltpu.VMEM((n, feats + samples, TB), jnp.bfloat16),
            pltpu.VMEM((PADDED, points), jnp.bfloat16),
            pltpu.VMEM((TB, PADDED), jnp.bfloat16),
            pltpu.VMEM((rows, samples, TB), jnp.float32),
            pltpu.VMEM((rows, n, TB), jnp.float32),
            pltpu.VMEM((TB, TB), jnp.bfloat16),
            pltpu.VMEM((TB, TB), jnp.bfloat16),
            pltpu.SemaphoreType.DMA((copies,)),
            pltpu.SemaphoreType.DMA((n,)),
            pltpu.SemaphoreType.DMA((copies,)),
            pltpu.SemaphoreType.DMA((n,)),
        ],
        compiler_params=pltpu.CompilerParams(
            collective_id=1, has_side_effects=True, vmem_limit_bytes=56 * 2**20
        ),
        name="samples",
    )(
        test_points, train_points, update_columns, lengthscales[None, :], frequencies.T, phases,
        prior_weights.T, pattern.T,
    )


def on_device(
    test_points, train_points, update_columns, pattern, lengthscales, frequencies, phases,
    prior_weights,
):
    n = lax.axis_size("blk")
    feats, points = test_points.shape
    samples = update_columns.shape[0]
    depth = frequencies.shape[1]
    pack = jnp.concatenate(
        [
            frequencies.T, jnp.zeros((depth, feats), jnp.bfloat16), phases.T,
            jnp.zeros((depth, PADDED - 2 * feats - 1), jnp.bfloat16), prior_weights.T,
            jnp.zeros((depth, PADDED - samples), jnp.bfloat16),
        ],
        axis=1,
    )
    vmem = pl.BlockSpec(memory_space=pltpu.VMEM)
    copies = n // 4 + 1 + 2 * (n // 4 - 1) + n // 4
    train_aug, all_columns, test_aug, prior = pl.pallas_call(
        functools.partial(gather_kernel, n),
        out_shape=(
            jax.ShapeDtypeStruct((n, TB, PADDED), jnp.bfloat16),
            jax.ShapeDtypeStruct((n, samples, TB), jnp.bfloat16),
            jax.ShapeDtypeStruct((PADDED, points), jnp.bfloat16),
            jax.ShapeDtypeStruct((samples, points), jnp.float32),
        ),
        in_specs=[vmem] * 5,
        out_specs=(vmem,) * 4,
        scratch_shapes=[
            pltpu.VMEM((n, depth, 2 * PADDED), jnp.bfloat16),
            pltpu.VMEM((n, feats + samples, TB), jnp.bfloat16),
            pltpu.SemaphoreType.DMA((copies,)),
            pltpu.SemaphoreType.DMA((n,)),
            pltpu.SemaphoreType.DMA((copies,)),
            pltpu.SemaphoreType.DMA((n,)),
        ],
        compiler_params=pltpu.CompilerParams(
            collective_id=0, has_side_effects=True, vmem_limit_bytes=56 * 2**20
        ),
        name="gather_and_prior",
    )(test_points, train_points, update_columns, lengthscales[:, None], pack)
    return pl.pallas_call(
        tile_kernel,
        out_shape=jax.ShapeDtypeStruct((samples, points), jnp.float32),
        in_specs=[pl.BlockSpec(memory_space=pltpu.SMEM)] + [vmem] * 4,
        out_specs=vmem,
        scratch_shapes=[
            pltpu.VMEM((points // TB + 1, samples, TB), jnp.float32),
            pltpu.VMEM((TB, TB), jnp.bfloat16),
            pltpu.VMEM((TB, TB), jnp.bfloat16),
            pltpu.SMEM((points // TB * pattern.shape[1] + 2 * UNROLL,), jnp.int32),
            pltpu.SMEM((points // TB * pattern.shape[1] + 2 * UNROLL,), jnp.int32),
        ],
        compiler_params=pltpu.CompilerParams(vmem_limit_bytes=56 * 2**20),
        name="tiles",
    )(pattern, train_aug, all_columns, test_aug, prior)


def either(test_points, train_points, update_columns, pattern, *others):
    rows = test_points.shape[1] // TB
    dense = pattern.shape[1] >= lax.axis_size("blk") and rows % 2 == 0
    run = dense_on_device if dense else on_device
    return run(test_points, train_points, update_columns, pattern, *others)


def solution(mesh):
    placed = (
        P(None, ("groups", "blk")),
        P(None, ("groups", "blk")),
        P(None, ("groups", "blk")),
        P("groups", None),
        P("groups"),
        P(None, "blk"),
        P(None, "blk"),
        P(None, "blk"),
    )
    return jax.shard_map(
        either, mesh=mesh, in_specs=placed, out_specs=P(None, ("groups", "blk")), check_vma=False
    )
```

```python
import functools
import math

import jax
import jax.numpy as jnp
from jax import lax
from jax.experimental import pallas as pl
from jax.experimental.pallas import tpu as pltpu
from jax.sharding import PartitionSpec as P

TB = 512
PADDED = 128
MESH = pl.DeviceIdType.MESH
LOG2E = math.log2(math.e)
NORM = 5.0 / 3.0
COS_TERMS = [(-1.0) ** k * (2.0 * math.pi) ** (2 * k) / math.factorial(2 * k) for k in range(11)]


def three_parts(value):
    high = value.astype(jnp.bfloat16).astype(jnp.float32)
    rest = value - high
    middle = rest.astype(jnp.bfloat16).astype(jnp.float32)
    return high, middle, (rest - middle).astype(jnp.bfloat16).astype(jnp.float32)


def rows_of(first, second):
    width = first[0].shape[1] if hasattr(first[0], "shape") else second[0].shape[1]
    row = lax.broadcasted_iota(jnp.int32, (32, width), 0)
    out = jnp.zeros((32, width), jnp.float32)
    for place, part in enumerate(list(first) + list(second)):
        out = jnp.where(row == place, part, out)
    return out


def turn_cos(turns):
    f = turns - jnp.round(turns)
    z = f * f
    total = jnp.full_like(z, COS_TERMS[-1])
    for term in COS_TERMS[-2::-1]:
        total = total * z + term
    return total


def gather_kernel(
    n, test_ref, train_ref, columns_ref, scale_ref, pack_ref,
    train_aug, all_columns, test_aug, prior_ref,
    packs, blocks, small_send, small_recv, big_send, big_recv,
):
    group = lax.axis_index("groups")
    me = lax.axis_index("blk")
    feats, samples = train_ref.shape[0], columns_ref.shape[0]
    depth = pack_ref.shape[0]
    lines = n // 4
    a, b, c = me // 4, (me // 2) % 2, me % 2

    def index(a_, b_, c_):
        return (a_ * 2 + b_) * 2 + c_

    line = [index((a + k) % lines, b, c) for k in range(lines)]
    across = index(a, 1 - b, c)
    core = index(a, b, 1 - c)
    partners = line[1:] + [across, core]

    barrier = pltpu.get_barrier_semaphore()
    for other in partners:
        pl.semaphore_signal(barrier, inc=1, device_id=(group, other), device_id_type=MESH)

    scale = scale_ref[...]
    train = (train_ref[...].astype(jnp.float32) / scale).astype(jnp.bfloat16)
    blocks[pl.ds(me, 1), :feats, :] = train[None]
    blocks[pl.ds(me, 1), feats:, :] = columns_ref[...][None]
    packs[pl.ds(me, 1)] = pack_ref[...][None]
    pl.semaphore_wait(barrier, len(partners))

    def copy(buffer, send, recv, source, target, number):
        return pltpu.make_async_remote_copy(
            src_ref=buffer.at[pl.ds(source, 1)], dst_ref=buffer.at[pl.ds(source, 1)],
            send_sem=send.at[number], recv_sem=recv.at[source],
            device_id=(group, target), device_id_type=MESH,
        )

    sent = []

    def start(small, source, target):
        number = counts[small]
        counts[small] += 1
        one = (copy(packs, small_send, small_recv, source, target, number) if small
               else copy(blocks, big_send, big_recv, source, target, number))
        one.start()
        sent.append(one)

    def arrive(small, source):
        if small:
            copy(packs, small_send, small_recv, source, me, 0).wait_recv()
        else:
            copy(blocks, big_send, big_recv, source, me, 0).wait_recv()

    counts = {True: 0, False: 0}

    def first_wave(small):
        for other in line[1:]:
            start(small, me, other)
        start(small, me, across)
        start(small, me, core)

    def line_arrivals(small):
        for k in range(1, lines):
            source = line[lines - k]
            arrive(small, source)
            start(small, source, across)
            start(small, source, core)

    def across_arrivals(small):
        for k in range(lines):
            source = index((a - k) % lines, 1 - b, c)
            arrive(small, source)
            start(small, source, core)

    def core_arrivals(small):
        for k in range(lines):
            arrive(small, index((a - k) % lines, b, 1 - c))
            arrive(small, index((a - k) % lines, 1 - b, 1 - c))

    first_wave(True)
    first_wave(False)

    chunks = test_ref.shape[1] // TB

    def make_test(i, _):
        at = pl.ds(pl.multiple_of(i * TB, TB), TB)
        scaled = (test_ref[:, at].astype(jnp.float32) / scale).astype(jnp.bfloat16)
        wide = scaled.astype(jnp.float32)
        norm = NORM * jnp.sum(wide * wide, axis=0, keepdims=True)
        tail = rows_of([1.0, 1.0, 1.0], three_parts(norm))
        test_aug[:feats, at] = scaled
        test_aug[feats:2 * feats, at] = scaled
        test_aug[2 * feats:, at] = tail.astype(jnp.bfloat16)
        return 0

    lax.fori_loop(0, chunks, make_test, 0)

    line_arrivals(True)
    across_arrivals(True)
    core_arrivals(True)
    line_arrivals(False)

    total = n * depth
    factor = math.sqrt(2.0 / total)
    step = min(total, 256)
    held = step // depth

    def make_prior(i, _):
        at = pl.ds(pl.multiple_of(i * TB, TB), TB)

        def part(first):
            pack = packs[pl.ds(first, held)].reshape(step, 2 * PADDED)
            turns = jnp.dot(
                pack[:, :PADDED], test_aug[:, at], preferred_element_type=jnp.float32
            ) * (0.5 / math.pi)
            features = turn_cos(turns).astype(jnp.bfloat16)
            return lax.dot_general(
                pack[:, PADDED:], features, (((0,), (0,)), ((), ())),
                preferred_element_type=jnp.float32,
            )[:samples]

        if total == step:
            result = part(0)
        else:
            result = lax.fori_loop(
                0, total // step, lambda p, run: run + part(p * held),
                jnp.zeros((samples, TB), jnp.float32),
            )
        prior_ref[:, at] = result * factor
        return 0

    lax.fori_loop(0, chunks, make_prior, 0)

    across_arrivals(False)
    core_arrivals(False)

    def make_train(s, _):
        block = blocks[pl.ds(s, 1)][0]
        wide = block[:feats].astype(jnp.float32)
        norm = NORM * jnp.sum(wide * wide, axis=0, keepdims=True)
        double = (-2.0 * NORM) * wide
        high = double.astype(jnp.bfloat16).astype(jnp.float32)
        tail = rows_of(three_parts(norm), [1.0, 1.0, 1.0])
        whole = jnp.concatenate([high, double - high, tail], axis=0)
        train_aug[pl.ds(s, 1)] = whole.T.astype(jnp.bfloat16)[None]
        all_columns[pl.ds(s, 1)] = block[feats:][None]
        return 0

    lax.fori_loop(0, n, make_train, 0)
    for one in sent:
        one.wait_send()


def matern(dist):
    dist = jnp.maximum(dist, 1e-30)
    w = dist * lax.rsqrt(dist)
    bell = jnp.exp2(w * (-LOG2E * math.sqrt(3.0)))
    return (((w + math.sqrt(3.0)) * w + 1.0) * bell).astype(jnp.bfloat16)


UNROLL = 4


def tile_kernel(
    pattern_ref, train_aug, all_columns, test_aug, prior_ref, out_ref,
    sums, even, odd, row_list, block_list,
):
    me = lax.axis_index("blk")
    rows = test_aug.shape[1] // TB
    slots = pattern_ref.shape[1]

    def list_row(row, count):
        def more(state):
            slot, _ = state
            return jnp.logical_and(
                slot < slots, pattern_ref[me * rows + row, jnp.minimum(slot, slots - 1)] >= 0
            )

        def put(state):
            slot, place = state
            row_list[place] = row
            block_list[place] = pattern_ref[me * rows + row, slot]
            return slot + 1, place + 1

        return lax.while_loop(more, put, (0, count))[1]

    count = lax.fori_loop(0, rows, list_row, 0)
    for extra in range(UNROLL + 1):
        row_list[count + extra] = rows
        block_list[count + extra] = 0
    sums[...] = jnp.zeros_like(sums)

    def front(place, held):
        row = jnp.minimum(row_list[place], rows - 1)
        at = pl.ds(pl.multiple_of(row * TB, TB), TB)
        held[...] = matern(jnp.dot(
            train_aug[block_list[place]], test_aug[:, at], preferred_element_type=jnp.float32
        ))

    def back(place, held):
        sums[row_list[place]] += jnp.dot(
            all_columns[block_list[place]], held[...], preferred_element_type=jnp.float32
        )

    held = (even, odd)
    front(0, even)

    def step(i, _):
        first = i * UNROLL
        for u in range(UNROLL):
            front(first + u + 1, held[(u + 1) % 2])
            back(first + u, held[u % 2])
        return 0

    lax.fori_loop(0, (count + UNROLL - 1) // UNROLL, step, 0)
    for row in range(rows):
        at = pl.ds(row * TB, TB)
        out_ref[:, at] = prior_ref[:, at] + sums[row]


def as_column(row):
    size = row.shape[1]
    across = lax.broadcasted_iota(jnp.int32, (size, size), 1)
    down = lax.broadcasted_iota(jnp.int32, (size, size), 0)
    return jnp.sum(jnp.where(across == down, row, 0.0), axis=1, keepdims=True)


def dense_kernel(
    n, test_ref, train_ref, columns_ref, scale_ref, freq_ref, phase_ref, weight_ref, pattern_ref,
    out_ref,
    packs, blocks, test_aug, train_aug, sums, masks, even, odd,
    small_send, small_recv, big_send, big_recv,
):
    group = lax.axis_index("groups")
    me = lax.axis_index("blk")
    feats, samples = train_ref.shape[0], columns_ref.shape[0]
    depth = freq_ref.shape[0]
    rows = test_ref.shape[1] // TB
    lines = n // 4
    a, b, c = me // 4, (me // 2) % 2, me % 2

    def index(a_, b_, c_):
        return (a_ * 2 + b_) * 2 + c_

    line = [index((a + k) % lines, b, c) for k in range(lines)]
    across = index(a, 1 - b, c)
    core = index(a, b, 1 - c)
    partners = [core, across] + line[1:]

    barrier = pltpu.get_barrier_semaphore()
    for other in partners:
        pl.semaphore_signal(barrier, inc=1, device_id=(group, other), device_id_type=MESH)

    scale = as_column(scale_ref[...])
    train = (train_ref[...].astype(jnp.float32) / scale).astype(jnp.bfloat16)
    blocks[pl.ds(me, 1), :feats, :] = train[None]
    blocks[pl.ds(me, 1), feats:, :] = columns_ref[...][None]
    lane = lax.broadcasted_iota(jnp.int32, (depth, PADDED), 1)
    phase = as_column(phase_ref[...].astype(jnp.float32))
    pack = jnp.where(lane == 2 * feats, phase, 0.0).astype(jnp.bfloat16)
    packs[pl.ds(me, 1), :, :PADDED] = pack[None]
    packs[pl.ds(me, 1), :, :feats] = freq_ref[...][None]
    packs[pl.ds(me, 1), :, PADDED:] = jnp.zeros((1, depth, PADDED), jnp.bfloat16)
    packs[pl.ds(me, 1), :, PADDED:PADDED + samples] = weight_ref[...][None]
    pl.semaphore_wait(barrier, len(partners))

    def copy(buffer, send, recv, source, target, number):
        return pltpu.make_async_remote_copy(
            src_ref=buffer.at[pl.ds(source, 1)], dst_ref=buffer.at[pl.ds(source, 1)],
            send_sem=send.at[number], recv_sem=recv.at[source],
            device_id=(group, target), device_id_type=MESH,
        )

    def small(source, target, number):
        return copy(packs, small_send, small_recv, source, target, number)

    def big(source, target, number):
        return copy(blocks, big_send, big_recv, source, target, number)

    for number, other in enumerate(partners):
        small(me, other, number).start()
    for number, other in enumerate(partners):
        big(me, other, number).start()
    copies = 4 * lines - 1

    def make_test(i, _):
        at = pl.ds(pl.multiple_of(i * TB, TB), TB)
        scaled = (test_ref[:, at].astype(jnp.float32) / scale).astype(jnp.bfloat16)
        wide = scaled.astype(jnp.float32)
        norm = NORM * jnp.sum(wide * wide, axis=0, keepdims=True)
        tail = rows_of([1.0, 1.0, 1.0], three_parts(norm))
        test_aug[:feats, at] = scaled
        test_aug[feats:2 * feats, at] = scaled
        test_aug[2 * feats:, at] = tail.astype(jnp.bfloat16)
        return 0

    lax.fori_loop(0, rows, make_test, 0)

    slots, all_rows = pattern_ref.shape
    wide_pattern = pattern_ref[...].astype(jnp.float32)
    place = lax.broadcasted_iota(jnp.int32, (slots, all_rows), 1)
    number = lax.broadcasted_iota(jnp.int32, (slots, n), 1).astype(jnp.float32)
    for row in range(rows):
        named = jnp.sum(
            jnp.where(place == me * rows + row, wide_pattern, 0.0), axis=1, keepdims=True
        )
        found = jnp.sum(jnp.where(named == number, 1.0, 0.0), axis=0, keepdims=True)
        masks[row] = jnp.broadcast_to(as_column(found), (n, TB))

    sums[...] = jnp.zeros_like(sums)
    odd[...] = jnp.zeros_like(odd)
    held = (even, odd)

    def kind_and_far(k):
        rest = k - 3
        kind = jnp.where(k < 3, (2 * k) % 3, jnp.minimum(rest // (lines - 1), 3))
        far = jnp.where(k < 3, 0, rest - kind * (lines - 1) + jnp.where(kind < 3, 1, 0))
        return kind, far

    def origin(k):
        kind, far = kind_and_far(k)
        swap_b, swap_c = kind % 2, kind // 2
        return index(
            (a + lines - far) % lines, b + swap_b - 2 * b * swap_b, c + swap_c - 2 * c * swap_c
        )

    def front(row):
        at = pl.ds(row * TB, TB)
        held[row % 2][...] = matern(
            jnp.dot(train_aug[...], test_aug[:, at], preferred_element_type=jnp.float32)
        )

    def back(source, row):
        product = jnp.dot(
            blocks[pl.ds(source, 1), feats:, :][0], held[row % 2][...],
            preferred_element_type=jnp.float32,
        )
        sums[row] += product * masks[row, pl.ds(source, 1), :]

    def one_block(k, _):
        source = origin(k)
        before = origin(jnp.maximum(k - 1, 0))

        @pl.when(k > 0)
        def _():
            big(source, me, 0).wait_recv()

        kind, far = kind_and_far(k)

        @pl.when(jnp.logical_and(kind == 0, k > 0))
        def _():
            big(source, across, lines + 2 * far - 1).start()
            big(source, core, lines + 2 * far).start()
            small(source, me, 0).wait_recv()
            small(source, across, lines + 2 * far - 1).start()
            small(source, core, lines + 2 * far).start()

        @pl.when(kind == 1)
        def _():
            big(source, core, 3 * lines - 1 + far).start()
            small(source, me, 0).wait_recv()
            small(source, core, 3 * lines - 1 + far).start()

        @pl.when(kind >= 2)
        def _():
            small(source, me, 0).wait_recv()

        wide = blocks[pl.ds(source, 1), :feats, :][0].astype(jnp.float32)
        norm = NORM * jnp.sum(wide * wide, axis=0, keepdims=True)
        double = (-2.0 * NORM) * wide
        high = double.astype(jnp.bfloat16).astype(jnp.float32)
        tail = rows_of(three_parts(norm), [1.0, 1.0, 1.0])
        whole = jnp.concatenate([high, double - high, tail], axis=0)
        train_aug[...] = whole.T.astype(jnp.bfloat16)
        for row in range(rows):
            front(row)
            if row == 0:
                back(before, rows - 1)
            else:
                back(source, row - 1)
        return 0

    lax.fori_loop(0, n, one_block, 0)
    back(origin(n - 1), rows - 1)

    factor = math.sqrt(2.0 / (n * depth))
    every = packs[...].reshape(n * depth, 2 * PADDED)

    def finish(i, _):
        at = pl.ds(pl.multiple_of(i * TB, TB), TB)
        turns = jnp.dot(
            every[:, :PADDED], test_aug[:, at], preferred_element_type=jnp.float32
        ) * (0.5 / math.pi)
        prior = lax.dot_general(
            every[:, PADDED:], turn_cos(turns).astype(jnp.bfloat16), (((0,), (0,)), ((), ())),
            preferred_element_type=jnp.float32,
        )[:samples]
        out_ref[:, at] = prior * factor + sums[pl.ds(i, 1)][0]
        return 0

    lax.fori_loop(0, rows, finish, 0)
    for number in range(copies):
        small(me, core, number).wait_send()
        big(me, core, number).wait_send()


def dense_on_device(
    test_points, train_points, update_columns, pattern, lengthscales, frequencies, phases,
    prior_weights,
):
    n = lax.axis_size("blk")
    feats, points = test_points.shape
    samples = update_columns.shape[0]
    depth = frequencies.shape[1]
    rows = points // TB
    vmem = pl.BlockSpec(memory_space=pltpu.VMEM)
    copies = n - 1
    return pl.pallas_call(
        functools.partial(dense_kernel, n),
        out_shape=jax.ShapeDtypeStruct((samples, points), jnp.float32),
        in_specs=[vmem] * 8,
        out_specs=vmem,
        scratch_shapes=[
            pltpu.VMEM((n, depth, 2 * PADDED), jnp.bfloat16),
            pltpu.VMEM((n, feats + samples, TB), jnp.bfloat16),
            pltpu.VMEM((PADDED, points), jnp.bfloat16),
            pltpu.VMEM((TB, PADDED), jnp.bfloat16),
            pltpu.VMEM((rows, samples, TB), jnp.float32),
            pltpu.VMEM((rows, n, TB), jnp.float32),
            pltpu.VMEM((TB, TB), jnp.bfloat16),
            pltpu.VMEM((TB, TB), jnp.bfloat16),
            pltpu.SemaphoreType.DMA((copies,)),
            pltpu.SemaphoreType.DMA((n,)),
            pltpu.SemaphoreType.DMA((copies,)),
            pltpu.SemaphoreType.DMA((n,)),
        ],
        compiler_params=pltpu.CompilerParams(
            collective_id=1, has_side_effects=True, vmem_limit_bytes=56 * 2**20
        ),
        name="samples",
    )(
        test_points, train_points, update_columns, lengthscales[None, :], frequencies.T, phases,
        prior_weights.T, pattern.T,
    )


def on_device(
    test_points, train_points, update_columns, pattern, lengthscales, frequencies, phases,
    prior_weights,
):
    n = lax.axis_size("blk")
    feats, points = test_points.shape
    samples = update_columns.shape[0]
    depth = frequencies.shape[1]
    pack = jnp.concatenate(
        [
            frequencies.T, jnp.zeros((depth, feats), jnp.bfloat16), phases.T,
            jnp.zeros((depth, PADDED - 2 * feats - 1), jnp.bfloat16), prior_weights.T,
            jnp.zeros((depth, PADDED - samples), jnp.bfloat16),
        ],
        axis=1,
    )
    vmem = pl.BlockSpec(memory_space=pltpu.VMEM)
    copies = n // 4 + 1 + 2 * (n // 4 - 1) + n // 4
    train_aug, all_columns, test_aug, prior = pl.pallas_call(
        functools.partial(gather_kernel, n),
        out_shape=(
            jax.ShapeDtypeStruct((n, TB, PADDED), jnp.bfloat16),
            jax.ShapeDtypeStruct((n, samples, TB), jnp.bfloat16),
            jax.ShapeDtypeStruct((PADDED, points), jnp.bfloat16),
            jax.ShapeDtypeStruct((samples, points), jnp.float32),
        ),
        in_specs=[vmem] * 5,
        out_specs=(vmem,) * 4,
        scratch_shapes=[
            pltpu.VMEM((n, depth, 2 * PADDED), jnp.bfloat16),
            pltpu.VMEM((n, feats + samples, TB), jnp.bfloat16),
            pltpu.SemaphoreType.DMA((copies,)),
            pltpu.SemaphoreType.DMA((n,)),
            pltpu.SemaphoreType.DMA((copies,)),
            pltpu.SemaphoreType.DMA((n,)),
        ],
        compiler_params=pltpu.CompilerParams(
            collective_id=0, has_side_effects=True, vmem_limit_bytes=56 * 2**20
        ),
        name="gather_and_prior",
    )(test_points, train_points, update_columns, lengthscales[:, None], pack)
    return pl.pallas_call(
        tile_kernel,
        out_shape=jax.ShapeDtypeStruct((samples, points), jnp.float32),
        in_specs=[pl.BlockSpec(memory_space=pltpu.SMEM)] + [vmem] * 4,
        out_specs=vmem,
        scratch_shapes=[
            pltpu.VMEM((points // TB + 1, samples, TB), jnp.float32),
            pltpu.VMEM((TB, TB), jnp.bfloat16),
            pltpu.VMEM((TB, TB), jnp.bfloat16),
            pltpu.SMEM((points // TB * pattern.shape[1] + 2 * UNROLL,), jnp.int32),
            pltpu.SMEM((points // TB * pattern.shape[1] + 2 * UNROLL,), jnp.int32),
        ],
        compiler_params=pltpu.CompilerParams(vmem_limit_bytes=56 * 2**20),
        name="tiles",
    )(pattern, train_aug, all_columns, test_aug, prior)


def either(test_points, train_points, update_columns, pattern, *others):
    rows = test_points.shape[1] // TB
    dense = pattern.shape[1] >= lax.axis_size("blk") and rows % 2 == 0
    run = dense_on_device if dense else on_device
    return run(test_points, train_points, update_columns, pattern, *others)


def solution(mesh):
    placed = (
        P(None, ("groups", "blk")),
        P(None, ("groups", "blk")),
        P(None, ("groups", "blk")),
        P("groups", None),
        P("groups"),
        P(None, "blk"),
        P(None, "blk"),
        P(None, "blk"),
    )
    return jax.shard_map(
        either, mesh=mesh, in_specs=placed, out_specs=P(None, ("groups", "blk")), check_vma=False
    )
```

```python
import functools
import math

import jax
import jax.numpy as jnp
from jax import lax
from jax.experimental import pallas as pl
from jax.experimental.pallas import tpu as pltpu
from jax.sharding import PartitionSpec as P

TB = 512
PADDED = 128
MESH = pl.DeviceIdType.MESH
LOG2E = math.log2(math.e)
NORM = 5.0 / 3.0
SIN_TERMS = [
    (-1.0) ** k * (2.0 * math.pi) ** (2 * k + 1) / math.factorial(2 * k + 1) for k in range(7)
]


def three_parts(value):
    high = value.astype(jnp.bfloat16).astype(jnp.float32)
    rest = value - high
    middle = rest.astype(jnp.bfloat16).astype(jnp.float32)
    return high, middle, (rest - middle).astype(jnp.bfloat16).astype(jnp.float32)


def rows_of(first, second):
    width = first[0].shape[1] if hasattr(first[0], "shape") else second[0].shape[1]
    row = lax.broadcasted_iota(jnp.int32, (32, width), 0)
    out = jnp.zeros((32, width), jnp.float32)
    for place, part in enumerate(list(first) + list(second)):
        out = jnp.where(row == place, part, out)
    return out


def turn_cos(turns):
    g = 0.25 - jnp.abs(turns - jnp.round(turns))
    z = g * g
    total = z * SIN_TERMS[-1] + SIN_TERMS[-2]
    for term in SIN_TERMS[-3::-1]:
        total = total * z + term
    return total * g


def gather_kernel(
    n, test_ref, train_ref, columns_ref, scale_ref, pack_ref,
    train_aug, all_columns, test_aug, prior_ref,
    packs, blocks, small_send, small_recv, big_send, big_recv,
):
    group = lax.axis_index("groups")
    me = lax.axis_index("blk")
    feats, samples = train_ref.shape[0], columns_ref.shape[0]
    depth = pack_ref.shape[0]
    lines = n // 4
    a, b, c = me // 4, (me // 2) % 2, me % 2

    def index(a_, b_, c_):
        return (a_ * 2 + b_) * 2 + c_

    line = [index((a + k) % lines, b, c) for k in range(lines)]
    across = index(a, 1 - b, c)
    core = index(a, b, 1 - c)
    partners = line[1:] + [across, core]

    barrier = pltpu.get_barrier_semaphore()
    for other in partners:
        pl.semaphore_signal(barrier, inc=1, device_id=(group, other), device_id_type=MESH)

    scale = scale_ref[...]
    train = (train_ref[...].astype(jnp.float32) / scale).astype(jnp.bfloat16)
    blocks[pl.ds(me, 1), :feats, :] = train[None]
    blocks[pl.ds(me, 1), feats:, :] = columns_ref[...][None]
    packs[pl.ds(me, 1)] = pack_ref[...][None]
    pl.semaphore_wait(barrier, len(partners))

    def copy(buffer, send, recv, source, target, number):
        return pltpu.make_async_remote_copy(
            src_ref=buffer.at[pl.ds(source, 1)], dst_ref=buffer.at[pl.ds(source, 1)],
            send_sem=send.at[number], recv_sem=recv.at[source],
            device_id=(group, target), device_id_type=MESH,
        )

    sent = []

    def start(small, source, target):
        number = counts[small]
        counts[small] += 1
        one = (copy(packs, small_send, small_recv, source, target, number) if small
               else copy(blocks, big_send, big_recv, source, target, number))
        one.start()
        sent.append(one)

    def arrive(small, source):
        if small:
            copy(packs, small_send, small_recv, source, me, 0).wait_recv()
        else:
            copy(blocks, big_send, big_recv, source, me, 0).wait_recv()

    counts = {True: 0, False: 0}

    def first_wave(small):
        for other in line[1:]:
            start(small, me, other)
        start(small, me, across)
        start(small, me, core)

    def line_arrivals(small):
        for k in range(1, lines):
            source = line[lines - k]
            arrive(small, source)
            start(small, source, across)
            start(small, source, core)

    def across_arrivals(small):
        for k in range(lines):
            source = index((a - k) % lines, 1 - b, c)
            arrive(small, source)
            start(small, source, core)

    def core_arrivals(small):
        for k in range(lines):
            arrive(small, index((a - k) % lines, b, 1 - c))
            arrive(small, index((a - k) % lines, 1 - b, 1 - c))

    first_wave(True)
    first_wave(False)

    chunks = test_ref.shape[1] // TB

    def make_test(i, _):
        at = pl.ds(pl.multiple_of(i * TB, TB), TB)
        scaled = (test_ref[:, at].astype(jnp.float32) / scale).astype(jnp.bfloat16)
        wide = scaled.astype(jnp.float32)
        norm = NORM * jnp.sum(wide * wide, axis=0, keepdims=True)
        tail = rows_of([1.0, 1.0, 1.0], three_parts(norm))
        test_aug[:feats, at] = scaled
        test_aug[feats:2 * feats, at] = scaled
        test_aug[2 * feats:, at] = tail.astype(jnp.bfloat16)
        return 0

    lax.fori_loop(0, chunks, make_test, 0)

    line_arrivals(True)
    across_arrivals(True)
    core_arrivals(True)
    line_arrivals(False)

    total = n * depth
    factor = math.sqrt(2.0 / total)
    step = min(total, 256)
    held = step // depth

    def make_prior(i, _):
        at = pl.ds(pl.multiple_of(i * TB, TB), TB)

        def part(first):
            pack = packs[pl.ds(first, held)].reshape(step, 2 * PADDED)
            turns = jnp.dot(
                pack[:, :PADDED], test_aug[:, at], preferred_element_type=jnp.float32
            ) * (0.5 / math.pi)
            features = turn_cos(turns).astype(jnp.bfloat16)
            return lax.dot_general(
                pack[:, PADDED:], features, (((0,), (0,)), ((), ())),
                preferred_element_type=jnp.float32,
            )[:samples]

        if total == step:
            result = part(0)
        else:
            result = lax.fori_loop(
                0, total // step, lambda p, run: run + part(p * held),
                jnp.zeros((samples, TB), jnp.float32),
            )
        prior_ref[:, at] = result * factor
        return 0

    lax.fori_loop(0, chunks, make_prior, 0)

    across_arrivals(False)
    core_arrivals(False)

    def make_train(s, _):
        block = blocks[pl.ds(s, 1)][0]
        wide = block[:feats].astype(jnp.float32)
        norm = NORM * jnp.sum(wide * wide, axis=0, keepdims=True)
        double = (-2.0 * NORM) * wide
        high = double.astype(jnp.bfloat16).astype(jnp.float32)
        tail = rows_of(three_parts(norm), [1.0, 1.0, 1.0])
        whole = jnp.concatenate([high, double - high, tail], axis=0)
        train_aug[pl.ds(s, 1)] = whole.T.astype(jnp.bfloat16)[None]
        all_columns[pl.ds(s, 1)] = block[feats:][None]
        return 0

    lax.fori_loop(0, n, make_train, 0)
    for one in sent:
        one.wait_send()


def matern(dist):
    dist = jnp.maximum(dist, 1e-30)
    w = dist * lax.rsqrt(dist)
    bell = jnp.exp2(w * (-LOG2E * math.sqrt(3.0)))
    return ((dist + (w * math.sqrt(3.0) + 1.0)) * bell).astype(jnp.bfloat16)


UNROLL = 4


def tile_kernel(
    pattern_ref, train_aug, all_columns, test_aug, prior_ref, out_ref,
    sums, even, odd, row_list, block_list,
):
    me = lax.axis_index("blk")
    rows = test_aug.shape[1] // TB
    slots = pattern_ref.shape[1]

    def list_row(row, count):
        def more(state):
            slot, _ = state
            return jnp.logical_and(
                slot < slots, pattern_ref[me * rows + row, jnp.minimum(slot, slots - 1)] >= 0
            )

        def put(state):
            slot, place = state
            row_list[place] = row
            block_list[place] = pattern_ref[me * rows + row, slot]
            return slot + 1, place + 1

        return lax.while_loop(more, put, (0, count))[1]

    count = lax.fori_loop(0, rows, list_row, 0)
    for extra in range(UNROLL + 1):
        row_list[count + extra] = rows
        block_list[count + extra] = 0
    sums[...] = jnp.zeros_like(sums)

    def front(place, held):
        row = jnp.minimum(row_list[place], rows - 1)
        at = pl.ds(pl.multiple_of(row * TB, TB), TB)
        held[...] = matern(jnp.dot(
            train_aug[block_list[place]], test_aug[:, at], preferred_element_type=jnp.float32
        ))

    def back(place, held):
        sums[row_list[place]] += jnp.dot(
            all_columns[block_list[place]], held[...], preferred_element_type=jnp.float32
        )

    held = (even, odd)
    front(0, even)

    def step(i, _):
        first = i * UNROLL
        for u in range(UNROLL):
            front(first + u + 1, held[(u + 1) % 2])
            back(first + u, held[u % 2])
        return 0

    lax.fori_loop(0, (count + UNROLL - 1) // UNROLL, step, 0)
    for row in range(rows):
        at = pl.ds(row * TB, TB)
        out_ref[:, at] = prior_ref[:, at] + sums[row]


def as_column(row):
    size = row.shape[1]
    across = lax.broadcasted_iota(jnp.int32, (size, size), 1)
    down = lax.broadcasted_iota(jnp.int32, (size, size), 0)
    return jnp.sum(jnp.where(across == down, row, 0.0), axis=1, keepdims=True)


def dense_kernel(
    n, test_ref, train_ref, columns_ref, scale_ref, freq_ref, phase_ref, weight_ref, pattern_ref,
    out_ref,
    packs, blocks, test_aug, train_aug, sums, masks, even, odd,
    small_send, small_recv, big_send, big_recv,
):
    group = lax.axis_index("groups")
    me = lax.axis_index("blk")
    feats, samples = train_ref.shape[0], columns_ref.shape[0]
    depth = freq_ref.shape[0]
    rows = test_ref.shape[1] // TB
    lines = n // 4
    a, b, c = me // 4, (me // 2) % 2, me % 2

    def index(a_, b_, c_):
        return (a_ * 2 + b_) * 2 + c_

    line = [index((a + k) % lines, b, c) for k in range(lines)]
    across = index(a, 1 - b, c)
    core = index(a, b, 1 - c)
    partners = [core, across] + line[1:]

    barrier = pltpu.get_barrier_semaphore()
    for other in partners:
        pl.semaphore_signal(barrier, inc=1, device_id=(group, other), device_id_type=MESH)

    scale = as_column(scale_ref[...])
    train = (train_ref[...].astype(jnp.float32) / scale).astype(jnp.bfloat16)
    blocks[pl.ds(me, 1), :feats, :] = train[None]
    blocks[pl.ds(me, 1), feats:, :] = columns_ref[...][None]
    lane = lax.broadcasted_iota(jnp.int32, (depth, PADDED), 1)
    phase = as_column(phase_ref[...].astype(jnp.float32))
    pack = jnp.where(lane == 2 * feats, phase, 0.0).astype(jnp.bfloat16)
    packs[pl.ds(me, 1), :, :PADDED] = pack[None]
    packs[pl.ds(me, 1), :, :feats] = freq_ref[...][None]
    packs[pl.ds(me, 1), :, PADDED:] = jnp.zeros((1, depth, PADDED), jnp.bfloat16)
    packs[pl.ds(me, 1), :, PADDED:PADDED + samples] = weight_ref[...][None]
    pl.semaphore_wait(barrier, len(partners))

    def copy(buffer, send, recv, source, target, number):
        return pltpu.make_async_remote_copy(
            src_ref=buffer.at[pl.ds(source, 1)], dst_ref=buffer.at[pl.ds(source, 1)],
            send_sem=send.at[number], recv_sem=recv.at[source],
            device_id=(group, target), device_id_type=MESH,
        )

    def small(source, target, number):
        return copy(packs, small_send, small_recv, source, target, number)

    def big(source, target, number):
        return copy(blocks, big_send, big_recv, source, target, number)

    for number, other in enumerate(partners):
        small(me, other, number).start()
    for number, other in enumerate(partners):
        big(me, other, number).start()
    copies = 4 * lines - 1

    def make_test(i, _):
        at = pl.ds(pl.multiple_of(i * TB, TB), TB)
        scaled = (test_ref[:, at].astype(jnp.float32) / scale).astype(jnp.bfloat16)
        wide = scaled.astype(jnp.float32)
        norm = NORM * jnp.sum(wide * wide, axis=0, keepdims=True)
        tail = rows_of([1.0, 1.0, 1.0], three_parts(norm))
        test_aug[:feats, at] = scaled
        test_aug[feats:2 * feats, at] = scaled
        test_aug[2 * feats:, at] = tail.astype(jnp.bfloat16)
        return 0

    lax.fori_loop(0, rows, make_test, 0)

    slots, all_rows = pattern_ref.shape
    wide_pattern = pattern_ref[...].astype(jnp.float32)
    place = lax.broadcasted_iota(jnp.int32, (slots, all_rows), 1)
    number = lax.broadcasted_iota(jnp.int32, (slots, n), 1).astype(jnp.float32)
    for row in range(rows):
        named = jnp.sum(
            jnp.where(place == me * rows + row, wide_pattern, 0.0), axis=1, keepdims=True
        )
        found = jnp.sum(jnp.where(named == number, 1.0, 0.0), axis=0, keepdims=True)
        masks[row] = jnp.broadcast_to(as_column(found), (n, TB))

    sums[...] = jnp.zeros_like(sums)
    odd[...] = jnp.zeros_like(odd)
    held = (even, odd)

    def kind_and_far(k):
        rest = k - 3
        kind = jnp.where(k < 3, (2 * k) % 3, jnp.minimum(rest // (lines - 1), 3))
        far = jnp.where(k < 3, 0, rest - kind * (lines - 1) + jnp.where(kind < 3, 1, 0))
        return kind, far

    def origin(k):
        kind, far = kind_and_far(k)
        swap_b, swap_c = kind % 2, kind // 2
        return index(
            (a + lines - far) % lines, b + swap_b - 2 * b * swap_b, c + swap_c - 2 * c * swap_c
        )

    def front(row):
        at = pl.ds(row * TB, TB)
        held[row % 2][...] = matern(
            jnp.dot(train_aug[...], test_aug[:, at], preferred_element_type=jnp.float32)
        )

    def back(source, row):
        product = jnp.dot(
            blocks[pl.ds(source, 1), feats:, :][0], held[row % 2][...],
            preferred_element_type=jnp.float32,
        )
        sums[row] += product * masks[row, pl.ds(source, 1), :]

    def one_block(k, _):
        source = origin(k)
        before = origin(jnp.maximum(k - 1, 0))

        @pl.when(k > 0)
        def _():
            big(source, me, 0).wait_recv()

        kind, far = kind_and_far(k)

        @pl.when(jnp.logical_and(kind == 0, k > 0))
        def _():
            big(source, across, lines + 2 * far - 1).start()
            big(source, core, lines + 2 * far).start()
            small(source, me, 0).wait_recv()
            small(source, across, lines + 2 * far - 1).start()
            small(source, core, lines + 2 * far).start()

        @pl.when(kind == 1)
        def _():
            big(source, core, 3 * lines - 1 + far).start()
            small(source, me, 0).wait_recv()
            small(source, core, 3 * lines - 1 + far).start()

        @pl.when(kind >= 2)
        def _():
            small(source, me, 0).wait_recv()

        wide = blocks[pl.ds(source, 1), :feats, :][0].astype(jnp.float32)
        norm = NORM * jnp.sum(wide * wide, axis=0, keepdims=True)
        double = (-2.0 * NORM) * wide
        high = double.astype(jnp.bfloat16).astype(jnp.float32)
        tail = rows_of(three_parts(norm), [1.0, 1.0, 1.0])
        whole = jnp.concatenate([high, double - high, tail], axis=0)
        train_aug[...] = whole.T.astype(jnp.bfloat16)
        for row in range(rows):
            front(row)
            if row == 0:
                back(before, rows - 1)
            else:
                back(source, row - 1)
        return 0

    lax.fori_loop(0, n, one_block, 0)
    back(origin(n - 1), rows - 1)

    factor = math.sqrt(2.0 / (n * depth))
    every = packs[...].reshape(n * depth, 2 * PADDED)

    def finish(i, _):
        at = pl.ds(pl.multiple_of(i * TB, TB), TB)
        turns = jnp.dot(
            every[:, :PADDED], test_aug[:, at], preferred_element_type=jnp.float32
        ) * (0.5 / math.pi)
        prior = lax.dot_general(
            every[:, PADDED:], turn_cos(turns).astype(jnp.bfloat16), (((0,), (0,)), ((), ())),
            preferred_element_type=jnp.float32,
        )[:samples]
        out_ref[:, at] = prior * factor + sums[pl.ds(i, 1)][0]
        return 0

    lax.fori_loop(0, rows, finish, 0)
    for number in range(copies):
        small(me, core, number).wait_send()
        big(me, core, number).wait_send()


def dense_on_device(
    test_points, train_points, update_columns, pattern, lengthscales, frequencies, phases,
    prior_weights,
):
    n = lax.axis_size("blk")
    feats, points = test_points.shape
    samples = update_columns.shape[0]
    depth = frequencies.shape[1]
    rows = points // TB
    vmem = pl.BlockSpec(memory_space=pltpu.VMEM)
    copies = n - 1
    return pl.pallas_call(
        functools.partial(dense_kernel, n),
        out_shape=jax.ShapeDtypeStruct((samples, points), jnp.float32),
        in_specs=[vmem] * 8,
        out_specs=vmem,
        scratch_shapes=[
            pltpu.VMEM((n, depth, 2 * PADDED), jnp.bfloat16),
            pltpu.VMEM((n, feats + samples, TB), jnp.bfloat16),
            pltpu.VMEM((PADDED, points), jnp.bfloat16),
            pltpu.VMEM((TB, PADDED), jnp.bfloat16),
            pltpu.VMEM((rows, samples, TB), jnp.float32),
            pltpu.VMEM((rows, n, TB), jnp.float32),
            pltpu.VMEM((TB, TB), jnp.bfloat16),
            pltpu.VMEM((TB, TB), jnp.bfloat16),
            pltpu.SemaphoreType.DMA((copies,)),
            pltpu.SemaphoreType.DMA((n,)),
            pltpu.SemaphoreType.DMA((copies,)),
            pltpu.SemaphoreType.DMA((n,)),
        ],
        compiler_params=pltpu.CompilerParams(
            collective_id=1, has_side_effects=True, vmem_limit_bytes=56 * 2**20
        ),
        name="samples",
    )(
        test_points, train_points, update_columns, lengthscales[None, :], frequencies.T, phases,
        prior_weights.T, pattern.T,
    )


def on_device(
    test_points, train_points, update_columns, pattern, lengthscales, frequencies, phases,
    prior_weights,
):
    n = lax.axis_size("blk")
    feats, points = test_points.shape
    samples = update_columns.shape[0]
    depth = frequencies.shape[1]
    pack = jnp.concatenate(
        [
            frequencies.T, jnp.zeros((depth, feats), jnp.bfloat16), phases.T,
            jnp.zeros((depth, PADDED - 2 * feats - 1), jnp.bfloat16), prior_weights.T,
            jnp.zeros((depth, PADDED - samples), jnp.bfloat16),
        ],
        axis=1,
    )
    vmem = pl.BlockSpec(memory_space=pltpu.VMEM)
    copies = n // 4 + 1 + 2 * (n // 4 - 1) + n // 4
    train_aug, all_columns, test_aug, prior = pl.pallas_call(
        functools.partial(gather_kernel, n),
        out_shape=(
            jax.ShapeDtypeStruct((n, TB, PADDED), jnp.bfloat16),
            jax.ShapeDtypeStruct((n, samples, TB), jnp.bfloat16),
            jax.ShapeDtypeStruct((PADDED, points), jnp.bfloat16),
            jax.ShapeDtypeStruct((samples, points), jnp.float32),
        ),
        in_specs=[vmem] * 5,
        out_specs=(vmem,) * 4,
        scratch_shapes=[
            pltpu.VMEM((n, depth, 2 * PADDED), jnp.bfloat16),
            pltpu.VMEM((n, feats + samples, TB), jnp.bfloat16),
            pltpu.SemaphoreType.DMA((copies,)),
            pltpu.SemaphoreType.DMA((n,)),
            pltpu.SemaphoreType.DMA((copies,)),
            pltpu.SemaphoreType.DMA((n,)),
        ],
        compiler_params=pltpu.CompilerParams(
            collective_id=0, has_side_effects=True, vmem_limit_bytes=56 * 2**20
        ),
        name="gather_and_prior",
    )(test_points, train_points, update_columns, lengthscales[:, None], pack)
    return pl.pallas_call(
        tile_kernel,
        out_shape=jax.ShapeDtypeStruct((samples, points), jnp.float32),
        in_specs=[pl.BlockSpec(memory_space=pltpu.SMEM)] + [vmem] * 4,
        out_specs=vmem,
        scratch_shapes=[
            pltpu.VMEM((points // TB + 1, samples, TB), jnp.float32),
            pltpu.VMEM((TB, TB), jnp.bfloat16),
            pltpu.VMEM((TB, TB), jnp.bfloat16),
            pltpu.SMEM((points // TB * pattern.shape[1] + 2 * UNROLL,), jnp.int32),
            pltpu.SMEM((points // TB * pattern.shape[1] + 2 * UNROLL,), jnp.int32),
        ],
        compiler_params=pltpu.CompilerParams(vmem_limit_bytes=56 * 2**20),
        name="tiles",
    )(pattern, train_aug, all_columns, test_aug, prior)


def either(test_points, train_points, update_columns, pattern, *others):
    rows = test_points.shape[1] // TB
    dense = pattern.shape[1] >= lax.axis_size("blk") and rows % 2 == 0
    run = dense_on_device if dense else on_device
    return run(test_points, train_points, update_columns, pattern, *others)


def solution(mesh):
    placed = (
        P(None, ("groups", "blk")),
        P(None, ("groups", "blk")),
        P(None, ("groups", "blk")),
        P("groups", None),
        P("groups"),
        P(None, "blk"),
        P(None, "blk"),
        P(None, "blk"),
    )
    return jax.shard_map(
        either, mesh=mesh, in_specs=placed, out_specs=P(None, ("groups", "blk")), check_vma=False
    )
```
